32 devices in a mesh: expert: 16 (over z, x, core), dp: 2 (over y).
Axes of the slice: x: 2, y: 2, z: 4, core: 2. Of those that a mesh axis runs over, the one named last changes fastest.
Arguments:
- tokens: bfloat16 [4096, 6144], P('expert', 'dp'), may hold values from -6 to 6
- grad_out: bfloat16 [4096, 6144], P('expert', 'dp'), may hold values from -0.625 to 0.625
- combine: bfloat16 [4096, 2], P('expert'), may hold values from 0.049804688 to 1
- routes: int32 [4096, 2], P('expert'), may hold values from 0 to 15, all different within a row; in each aligned block of 256 rows (0 to 255, 256 to 511, ...) at most 36 rows name the same one
- w_gate: bfloat16 [16, 256, 6144], P('expert', None, 'dp'), may hold values from -0.078125 to 0.078125
- w_up: bfloat16 [16, 256, 6144], P('expert', None, 'dp'), may hold values from -0.078125 to 0.078125
- w_down: bfloat16 [16, 256, 6144], P('expert', None, 'dp'), may hold values from -0.375 to 0.375
Outputs:
- grad_gate: bfloat16 [16, 256, 6144], P('expert', None, 'dp')
- grad_up: bfloat16 [16, 256, 6144], P('expert', None, 'dp')
- grad_down: bfloat16 [16, 256, 6144], P('expert', None, 'dp')
- grad_combine: float32 [4096, 2], P('expert')
The draws below stay inside these ranges and needn't reach their ends.
Inputs may be any that keep to these rules, and one draw needn't show every extreme that they name: `routes`: each token names 2 different experts. Among the tokens of one index of the expert axis no expert is named by more than 36 tokens, and on some index one expert is named by exactly 36 tokens.
All inputs are finite; a program needn't handle non-finite values.
Results may differ from the reference program's by a relative error of at most 0.0049.
Values may be sent and summed in bfloat16 or wider, within the bound.
A program may use at most 64 MiB of HBM per device.

```python
import math
import jax
import jax.numpy as jnp
import numpy as np
from jax import lax

D = 6144
FH = 256
TOP = 2
TOK = 256
EXPERTS = 16
TOKENS = 4096
MOST = 36
N_EXPERT = 16


def level_of(key, extent, shards, smallest, high):
    gain = 1.0
    for dim, parts in shards:
        heights = jax.random.uniform(jax.random.fold_in(jax.random.fold_in(key, 6), dim), (parts,), jnp.float32, smallest / len(shards), high / len(shards))
        gain = gain * jnp.repeat(jnp.exp(heights), extent[dim] // parts).reshape((-1,) + (1,) * (len(extent) - 1 - dim))
    return gain


def assign_block(own_key, own, number, rows, amount, top, most, lean):
    order = jax.random.permutation(own_key, amount)
    packed, ordinary = load_shares(amount, rows * top, most, lean, True), load_shares(amount, rows * top, most, lean, False)
    places = jnp.arange(amount)

    def named(sizes, offset_by):
        used = int((sizes > 0).sum())
        fixed = max(1, used // 4)
        shifted = fixed + (places - fixed + offset_by * (used - fixed)) % max(1, amount - fixed)
        return jnp.zeros((amount,), jnp.int32).at[order[jnp.where(places < fixed, places, shifted)]].set(jnp.asarray(sizes, jnp.int32))

    sizes = jnp.where(number % 4 == 0, named(packed, number // 4), named(ordinary, number - number // 4 - 1))
    mixed = jax.random.permutation(jax.random.fold_in(own, 3), amount)
    donor, sink = mixed[0:amount // 2 * 2:2], mixed[1:amount // 2 * 2:2]
    slack = jnp.minimum(sizes[donor] - 1, most - sizes[sink]) // 2
    slack = jnp.where((donor == order[0]) | (sink == order[0]) | (sizes[sink] == 0), 0, jnp.maximum(slack, 0))
    shifted = jax.random.randint(jax.random.fold_in(own, 4), (amount // 2,), 0, 1 << 20) % (slack + 1)
    sizes = sizes.at[donor].add(-shifted).at[sink].add(shifted)
    items = jnp.searchsorted(jnp.cumsum(sizes), jnp.arange(rows * top), side="right").astype(jnp.int32)
    grid = items.reshape(top, rows).T
    grid = grid[jax.random.permutation(jax.random.fold_in(own, 1), rows)]
    offset_by = jax.random.randint(jax.random.fold_in(own, 2), (rows, 1), 0, top)
    return jnp.take_along_axis(grid, (jnp.arange(top)[None, :] + offset_by) % top, axis=1)


def load_shares(count, total, bound, lean, full):
    portions = [(1 << 20) // math.isqrt(grade ** lean) + 1 for grade in range(1, count + 1)]
    largest = bound if full else min(bound, max(-(-total // count), total * portions[0] // sum(portions)))
    least = 1 if total - largest >= count - 1 else 0
    given, surplus = [largest] + [least] * (count - 1), total - largest - least * (count - 1)
    while surplus > 0:
        movable = [i for i in range(1, count) if given[i] < largest] or [i for i in range(1, count) if given[i] < bound]
        whole, left = sum([portions[i] for i in movable]), surplus
        for i in movable:
            extra = min(bound - given[i], max(1, left * portions[i] // whole), surplus)
            given[i] = given[i] + extra
            surplus = surplus - extra
    return np.array(given)


def normal_values(rng, shape, scale, bound, split=(), kind=jnp.bfloat16):
    gain = level_of(rng, shape, split, -0.22, 0.18) if split else 1.0
    array = jax.random.normal(rng, shape, jnp.float32) * scale * gain
    return jnp.minimum(jnp.maximum(array, -bound), bound).astype(kind)


def setup_inputs(seed: int = 0) -> dict:
    arg_keys = jax.random.split(jax.random.key(seed), 8)
    tokens = normal_values(arg_keys[0], (TOKENS, D), 1.0, 6.0, ((0, 16), (1, 2)))
    grad_out = normal_values(arg_keys[1], (TOKENS, D), ((TOK * TOP) ** -0.5), 0.625, ((0, 16), (1, 2)))
    combine = jnp.clip(0.049804688 + 0.9501953 * jax.random.uniform(arg_keys[2], (TOKENS, TOP), jnp.float32) ** level_of(arg_keys[2], (TOKENS, TOP), ((0, 16),), -0.2, 0.2), 0.049804688, 1.0).astype(jnp.bfloat16)
    routes_keys = jax.random.split(jax.random.fold_in(arg_keys[3], 1), TOKENS // TOK)
    routes_turns = jax.random.permutation(jax.random.fold_in(arg_keys[3], 3), TOKENS // TOK)
    routes = jax.vmap(lambda own, number: assign_block(jax.random.fold_in(arg_keys[3], 2), own, number, TOK, EXPERTS, TOP, MOST, 2))(routes_keys, routes_turns).reshape((TOKENS, TOP))
    w_gate = normal_values(arg_keys[4], (EXPERTS, FH, D), D ** -0.5, 0.078125, ((0, 16), (2, 2)))
    w_up = normal_values(arg_keys[5], (EXPERTS, FH, D), D ** -0.5, 0.078125, ((0, 16), (2, 2)))
    w_down = normal_values(arg_keys[6], (EXPERTS, FH, D), FH ** -0.5, 0.375, ((0, 16), (2, 2)))
    return {"tokens": tokens, "grad_out": grad_out, "combine": combine, "routes": routes, "w_gate": w_gate, "w_up": w_up, "w_down": w_down}


inner_dims = (((1,), (1,)), ((), ()))
outer_dims = (((0,), (0,)), ((), ()))


def silu_parts(gate_pre):
    sig_val = jax.nn.sigmoid(gate_pre)
    return gate_pre * sig_val, sig_val * (1.0 + gate_pre * (1.0 - sig_val))


def reference(tokens, grad_out, combine, routes, w_gate, w_up, w_down):
    assigned = TOKENS * TOP
    expert_cap = MOST * N_EXPERT
    flat_expert = routes.reshape(-1).astype(jnp.int32)
    token_of = (jnp.arange(assigned, dtype=jnp.int32) // TOP).astype(jnp.int32)
    flat_prob = combine.reshape(-1)
    ordering = jnp.argsort(flat_expert, stable=True).astype(jnp.int32)
    counts = jnp.zeros((EXPERTS,), jnp.int32).at[flat_expert].add(1)
    starts = (jnp.cumsum(counts) - counts).astype(jnp.int32)
    padded = jnp.concatenate([ordering, jnp.zeros((expert_cap,), jnp.int32)])

    def one_expert(expert):
        picked = lax.dynamic_slice(padded, (starts[expert],), (expert_cap,))
        valid = jnp.arange(expert_cap, dtype=jnp.int32) < counts[expert]
        rows_tok = token_of[picked]
        rows_x = tokens[rows_tok]
        rows_dy = grad_out[rows_tok]
        weight = jnp.where(valid, flat_prob[picked].astype(jnp.float32), jnp.float32(0.0))[:, None]
        gate_pre = lax.dot_general(rows_x, w_gate[expert], inner_dims, preferred_element_type=jnp.float32)
        up_pre = lax.dot_general(rows_x, w_up[expert], inner_dims, preferred_element_type=jnp.float32)
        grad_hid = lax.dot_general(rows_dy, w_down[expert], inner_dims, preferred_element_type=jnp.float32)
        silu_out, silu_slope = silu_parts(gate_pre)
        hidden = silu_out * up_pre
        weighted = (weight * hidden).astype(jnp.bfloat16)
        scaled = weight * grad_hid
        up_rows = (scaled * silu_out).astype(jnp.bfloat16)
        gate_rows = (scaled * up_pre * silu_slope).astype(jnp.bfloat16)
        scores = jnp.sum(hidden * grad_hid, axis=1)
        gate_grad = lax.dot_general(gate_rows, rows_x, outer_dims, preferred_element_type=jnp.float32)
        up_grad = lax.dot_general(up_rows, rows_x, outer_dims, preferred_element_type=jnp.float32)
        down_grad = lax.dot_general(weighted, rows_dy, outer_dims, preferred_element_type=jnp.float32)
        target = jnp.where(valid, picked, assigned).astype(jnp.int32)
        return gate_grad, up_grad, down_grad, scores, target

    gate_all, up_all, down_all, score_all, target_all = lax.map(one_expert, jnp.arange(EXPERTS, dtype=jnp.int32))
    grad_combine = jnp.zeros((assigned + 1,), jnp.float32).at[target_all.reshape(-1)].set(score_all.reshape(-1))
    grad_combine = grad_combine[:assigned].reshape(TOKENS, TOP)
    return (gate_all.astype(jnp.bfloat16), up_all.astype(jnp.bfloat16), down_all.astype(jnp.bfloat16), grad_combine)
```

```python
import functools

import jax
import jax.numpy as jnp
from jax import lax
from jax.experimental import pallas as pl
from jax.experimental.pallas import tpu as pltpu
from jax.sharding import PartitionSpec as P

MESH = pl.DeviceIdType.MESH
F32 = jnp.float32
BF16 = jnp.bfloat16


def round_up(value, unit):
    return (value + unit - 1) // unit * unit


def partner_of(me, k, n):
    out, bit = 0, 1
    while bit < n:
        out = out + (me // bit + k // bit) % 2 * bit
        bit *= 2
    return out


def diagonal(rows):
    return lax.broadcasted_iota(jnp.int32, (rows, 128), 0) == lax.broadcasted_iota(
        jnp.int32, (rows, 128), 1
    )


def to_row(col):
    rows = col.shape[0]
    return jnp.sum(jnp.where(diagonal(rows), col, 0.0), axis=0, keepdims=True)


def to_col(row, rows):
    return jnp.sum(jnp.where(diagonal(rows), row, 0.0), axis=1, keepdims=True)


def kernel(
    n, dp, cap, groups,
    slots_ref, prob_ref, tok_ref, dy_ref, wg_ref, wu_ref, wd_ref,
    gate_ref, up_ref, down_ref, comb_ref,
    msg, recv, w_all, rows_a, acc, parts, p_out, p_in, s_out, s_in,
    w_sem, m_send, m_recv, p_send, p_recv, s_send, s_recv, y_send, y_recv,
):
    me = lax.axis_index("expert")
    mine = lax.axis_index("dp")
    tok_count, width = tok_ref.shape
    hid = wg_ref.shape[1]
    pair = msg.shape[1]
    rows = parts.shape[2]

    def w_copy(i):
        src = (wg_ref, wu_ref, wd_ref)[i]
        return pltpu.make_async_copy(src.at[0], w_all.at[pl.ds(i * hid, hid)], w_sem.at[i])

    for i in range(3):
        w_copy(i).start()

    barrier = pltpu.get_barrier_semaphore()

    def greet(k, _):
        pl.semaphore_signal(
            barrier, inc=1, device_id=(partner_of(me, k, n), mine), device_id_type=MESH
        )
        return 0

    lax.fori_loop(1, n, greet, 0)
    for j in range(1, dp):
        pl.semaphore_signal(
            barrier, inc=1, device_id=(me, (mine + j) % dp), device_id_type=MESH
        )
    pl.semaphore_wait(barrier, n - 1 + dp - 1)

    def msg_copy(k):
        return pltpu.make_async_remote_copy(
            src_ref=msg.at[k], dst_ref=recv.at[k], send_sem=m_send.at[k], recv_sem=m_recv.at[k],
            device_id=(partner_of(me, k, n), mine), device_id_type=MESH,
        )

    def p_copy(k):
        return pltpu.make_async_remote_copy(
            src_ref=p_out.at[k], dst_ref=p_in.at[k], send_sem=p_send.at[k], recv_sem=p_recv.at[k],
            device_id=(partner_of(me, k, n), mine), device_id_type=MESH,
        )

    def s_copy(k):
        return pltpu.make_async_remote_copy(
            src_ref=s_out.at[k], dst_ref=s_in.at[k], send_sem=s_send.at[k], recv_sem=s_recv.at[k],
            device_id=(partner_of(me, k, n), mine), device_id_type=MESH,
        )

    def y_copy(j, k):
        return pltpu.make_async_remote_copy(
            src_ref=parts.at[mine, k], dst_ref=parts.at[mine, k],
            send_sem=y_send.at[j, k], recv_sem=y_recv.at[mine, k],
            device_id=(me, (mine + j) % dp), device_id_type=MESH,
        )

    def y_arrival(j, k):
        other = (mine + j) % dp
        return pltpu.make_async_remote_copy(
            src_ref=parts.at[other, k], dst_ref=parts.at[other, k],
            send_sem=y_send.at[j, k], recv_sem=y_recv.at[other, k],
            device_id=(me, other), device_id_type=MESH,
        )

    def build(k, msg_to, p_to):
        dest = partner_of(me, k, n)
        place = lax.broadcasted_iota(jnp.int32, (pair, tok_count), 0)
        first = slots_ref[0:1, :] - dest * cap
        second = slots_ref[1:2, :] - dest * cap
        is_x = place < cap
        is_dy = (place >= cap) & (place < 2 * cap)
        pick_x = is_x & ((first == place) | (second == place))
        pick_dy = is_dy & ((first + cap == place) | (second + cap == place))
        picked = jnp.dot(
            jnp.where(pick_x, 1.0, 0.0).astype(BF16), tok_ref[...], preferred_element_type=F32
        ) + jnp.dot(
            jnp.where(pick_dy, 1.0, 0.0).astype(BF16), dy_ref[...], preferred_element_type=F32
        )
        msg_to[k] = picked.astype(BF16)
        spot = lax.broadcasted_iota(jnp.int32, (rows, tok_count), 0)
        prob = jnp.where(first == spot, prob_ref[0:1, :], 0.0) + jnp.where(
            second == spot, prob_ref[1:2, :], 0.0
        )
        p_to[k] = jnp.broadcast_to(
            to_row(jnp.sum(prob, axis=1, keepdims=True)), p_to.shape[1:]
        )

    half = n // 2

    def send(i, _):
        k = (half + i) % n + i // half
        build(k, msg, p_out)
        p_copy(k).start()
        msg_copy(k).start()
        return 0

    lax.fori_loop(0, n - 1, send, 0)
    build(0, recv, p_in)
    for i in range(3):
        w_copy(i).wait()

    def project(k):
        both = lax.dot_general(
            recv[k], w_all[...], (((1,), (1,)), ((), ())), preferred_element_type=F32
        )
        parts[mine, k, :, 0 : 2 * hid] = both[0:rows, 0 : 2 * hid]
        parts[mine, k, :, 2 * hid : 3 * hid] = pltpu.roll(
            both[:, 2 * hid : 3 * hid], pair - cap, 0
        )[0:rows]
        for j in range(1, dp):
            y_copy(j, k).start()

    def combine_rows(k):
        for j in range(1, dp):
            y_arrival(j, k).wait_recv()
        total = parts[0, k]
        for r in range(1, dp):
            total = total + parts[r, k]
        gate_pre = total[:, 0:hid]
        up_pre = total[:, hid : 2 * hid]
        grad_hid = total[:, 2 * hid : 3 * hid]
        real = lax.broadcasted_iota(jnp.int32, (rows, hid), 0) < cap
        weight = to_col(p_in[k][0:1, :], rows)
        sig = jax.nn.sigmoid(gate_pre)
        silu_out = gate_pre * sig
        slope = sig * (1.0 + gate_pre * (1.0 - sig))
        hidden = silu_out * up_pre
        scaled = weight * grad_hid
        scores = jnp.sum(jnp.where(real, hidden * grad_hid, 0.0), axis=1, keepdims=True)

        def spread(value):
            value = jnp.where(real, value, 0.0)
            return jnp.concatenate([value, jnp.zeros((pair - rows, hid), F32)], axis=0)

        rows_a[k, :, 0:hid] = spread(scaled * up_pre * slope).astype(BF16)
        rows_a[k, :, hid : 2 * hid] = spread(scaled * silu_out).astype(BF16)
        rows_a[k, :, 2 * hid : 3 * hid] = pltpu.roll(
            spread(weight * hidden), cap, 0
        ).astype(BF16)
        return jnp.broadcast_to(to_row(scores), s_out.shape[1:])

    def finish(k):
        s_out[k] = combine_rows(k)
        s_copy(k).start()

    def step(k, _):
        msg_copy(k).wait_recv()
        project(k)
        p_copy(k - 1).wait_recv()
        finish(k - 1)
        return 0

    tile = 512 if width % 512 == 0 else 256

    def outer(lo, hi, opening, closing):
        depth = (hi - lo) * pair

        def columns(c, _):
            at = pl.ds(pl.multiple_of(c * tile, tile), tile)
            new = lax.dot_general(
                rows_a[lo:hi].reshape(depth, 3 * hid), recv[lo:hi, :, at].reshape(depth, tile),
                (((0,), (0,)), ((), ())), preferred_element_type=F32,
            )
            if not opening:
                new = new + acc[:, at]
            if closing:
                gate_ref[0, :, at] = new[0:hid].astype(BF16)
                up_ref[0, :, at] = new[hid : 2 * hid].astype(BF16)
                down_ref[0, :, at] = new[2 * hid : 3 * hid].astype(BF16)
            else:
                acc[:, at] = new
            return 0

        lax.fori_loop(0, width // tile, columns, 0)

    project(0)
    msg_copy(1).wait_recv()
    project(1)
    s_in[0] = combine_rows(0)
    done = 0
    at = 2
    for g, bound in enumerate(groups):
        last = bound == n
        lax.fori_loop(at, min(bound + 1, n), step, 0)
        at = min(bound + 1, n)
        if last:
            p_copy(n - 1).wait_recv()
            finish(n - 1)
        outer(done, bound, g == 0, last)
        done = bound

    def gather_scores(k, carry):
        one, two = carry
        spot = lax.broadcasted_iota(jnp.int32, (rows, tok_count), 0)
        spot = jnp.where(spot < cap, spot + partner_of(me, k, n) * cap, -1)
        col = to_col(s_in[k][0:1, :], rows)
        one = one + jnp.sum(jnp.where(slots_ref[0:1, :] == spot, col, 0.0), axis=0, keepdims=True)
        two = two + jnp.sum(jnp.where(slots_ref[1:2, :] == spot, col, 0.0), axis=0, keepdims=True)
        return one, two

    def arrived(k, carry):
        s_copy(k).wait_recv()
        return gather_scores(k, carry)

    zero = jnp.zeros((1, tok_count), F32)
    one, two = lax.fori_loop(1, n, arrived, gather_scores(0, (zero, zero)))
    comb_ref[0:1, :] = one
    comb_ref[1:2, :] = two

    def drain(k, _):
        msg_copy(k).wait_send()
        p_copy(k).wait_send()
        s_copy(k).wait_send()
        return 0

    lax.fori_loop(1, n, drain, 0)

    def drain_parts(k, _):
        for j in range(1, dp):
            y_copy(j, k).wait_send()
        return 0

    lax.fori_loop(0, n, drain_parts, 0)


def local(n, dp, tokens, grad_out, combine, routes, w_gate, w_up, w_down):
    tok_count, width = tokens.shape
    hid = w_gate.shape[1]
    top_count = routes.shape[1]
    cap = max(2, (9 * tok_count * top_count + 8 * n - 1) // (8 * n))
    flat_expert = routes.reshape(-1)
    onehot = (flat_expert[:, None] == jnp.arange(n, dtype=jnp.int32)[None, :]).astype(jnp.int32)
    before = jnp.cumsum(onehot, axis=0) - onehot
    ranking = jnp.sum(before * onehot, axis=1)
    slot_of = (flat_expert * cap + ranking).reshape(tok_count, top_count).T
    probs = combine.astype(F32).T
    pair = round_up(2 * cap, 8)
    rows = round_up(cap, 8)
    groups = (n // 2, 3 * n // 4, n)
    grad_shape = jax.ShapeDtypeStruct((1, hid, width), BF16)
    vmem = pl.BlockSpec(memory_space=pltpu.VMEM)
    hbm = pl.BlockSpec(memory_space=pl.ANY)
    dma = pltpu.SemaphoreType.DMA
    gate, up, down, comb = pl.pallas_call(
        functools.partial(kernel, n, dp, cap, groups),
        out_shape=(
            grad_shape, grad_shape, grad_shape,
            jax.ShapeDtypeStruct((top_count, tok_count), F32),
        ),
        in_specs=[vmem] * 4 + [hbm] * 3,
        out_specs=(vmem,) * 4,
        scratch_shapes=[
            pltpu.VMEM((n, pair, width), BF16),
            pltpu.VMEM((n, pair, width), BF16),
            pltpu.VMEM((3 * hid, width), BF16),
            pltpu.VMEM((n, pair, 3 * hid), BF16),
            pltpu.VMEM((3 * hid, width), F32),
            pltpu.VMEM((dp, n, rows, 3 * hid), F32),
            pltpu.VMEM((n, 8, 128), F32),
            pltpu.VMEM((n, 8, 128), F32),
            pltpu.VMEM((n, 8, 128), F32),
            pltpu.VMEM((n, 8, 128), F32),
            dma((3,)),
            dma((n,)), dma((n,)), dma((n,)), dma((n,)), dma((n,)), dma((n,)),
            dma((dp, n)), dma((dp, n)),
        ],
        compiler_params=pltpu.CompilerParams(
            collective_id=0, has_side_effects=True, vmem_limit_bytes=60 * 1024 * 1024
        ),
        cost_estimate=pl.CostEstimate(
            flops=12 * n * cap * hid * width, bytes_accessed=20 * hid * width, transcendentals=0
        ),
    )(slot_of, probs, tokens, grad_out, w_gate, w_up, w_down)
    return gate, up, down, comb.T


def solution(mesh):
    placed = (
        P("expert", "dp"),
        P("expert", "dp"),
        P("expert", None),
        P("expert", None),
        P("expert", None, "dp"),
        P("expert", None, "dp"),
        P("expert", None, "dp"),
    )
    return jax.shard_map(
        functools.partial(local, mesh.shape["expert"], mesh.shape["dp"]),
        mesh=mesh,
        in_specs=placed,
        out_specs=(
            P("expert", None, "dp"),
            P("expert", None, "dp"),
            P("expert", None, "dp"),
            P("expert", None),
        ),
        check_vma=False,
    )
```

```python
import functools

import jax
import jax.numpy as jnp
from jax import lax
from jax.experimental import pallas as pl
from jax.experimental.pallas import tpu as pltpu
from jax.sharding import PartitionSpec as P

MESH = pl.DeviceIdType.MESH
F32 = jnp.float32
BF16 = jnp.bfloat16


def round_up(value, unit):
    return (value + unit - 1) // unit * unit


def partner_of(me, k, n):
    out, bit = 0, 1
    while bit < n:
        out = out + (me // bit + k // bit) % 2 * bit
        bit *= 2
    return out


def diagonal(rows):
    return lax.broadcasted_iota(jnp.int32, (rows, 128), 0) == lax.broadcasted_iota(
        jnp.int32, (rows, 128), 1
    )


def to_row(col):
    rows = col.shape[0]
    return jnp.sum(jnp.where(diagonal(rows), col, 0.0), axis=0, keepdims=True)


def to_col(row, rows):
    return jnp.sum(jnp.where(diagonal(rows), row, 0.0), axis=1, keepdims=True)


def kernel(
    n, dp, cap, tile, ahead,
    routes_ref, prob_ref, tok_ref, dy_ref, wg_ref, wu_ref, wd_ref,
    gate_ref, up_ref, down_ref, comb_ref,
    slots_ref, msg, recv, staged, w_all, rows_a, acc, parts, p_out, p_in, s_out, s_in,
    w_sem, m_send, m_recv, p_send, p_recv, s_send, s_recv, y_send, y_recv, o_sem,
):
    me = lax.axis_index("expert")
    mine = lax.axis_index("dp")
    tok_count, width = tok_ref.shape
    hid = wg_ref.shape[1]
    pair = msg.shape[1]
    rows = parts.shape[2]
    half = n // 2

    def step_of(q):
        return q % 2 * half + q // 2

    def towards(q):
        return (partner_of(me, step_of(q), n), mine)

    def w_copy(i):
        src = (wg_ref, wu_ref, wd_ref)[i]
        return pltpu.make_async_copy(src.at[0], w_all.at[pl.ds(i * hid, hid)], w_sem.at[i])

    for i in range(3):
        w_copy(i).start()

    barrier = pltpu.get_barrier_semaphore()

    def greet(k, _):
        pl.semaphore_signal(
            barrier, inc=1, device_id=(partner_of(me, k, n), mine), device_id_type=MESH
        )
        return 0

    lax.fori_loop(1, n, greet, 0)
    for j in range(1, dp):
        pl.semaphore_signal(
            barrier, inc=1, device_id=(me, (mine + j) % dp), device_id_type=MESH
        )
    pl.semaphore_wait(barrier, n - 1 + dp - 1)

    def msg_copy(q):
        return pltpu.make_async_remote_copy(
            src_ref=msg.at[q], dst_ref=recv.at[q], send_sem=m_send.at[q], recv_sem=m_recv.at[q],
            device_id=towards(q), device_id_type=MESH,
        )

    def p_copy(q):
        return pltpu.make_async_remote_copy(
            src_ref=p_out.at[q], dst_ref=p_in.at[q], send_sem=p_send.at[q], recv_sem=p_recv.at[q],
            device_id=towards(q), device_id_type=MESH,
        )

    def s_copy(q):
        return pltpu.make_async_remote_copy(
            src_ref=s_out.at[q], dst_ref=s_in.at[q], send_sem=s_send.at[q], recv_sem=s_recv.at[q],
            device_id=towards(q), device_id_type=MESH,
        )

    def y_copy(j, k):
        return pltpu.make_async_remote_copy(
            src_ref=parts.at[mine, k], dst_ref=parts.at[mine, k],
            send_sem=y_send.at[j, k], recv_sem=y_recv.at[mine, k],
            device_id=(me, (mine + j) % dp), device_id_type=MESH,
        )

    def y_arrival(j, k):
        other = (mine + j) % dp
        return pltpu.make_async_remote_copy(
            src_ref=parts.at[other, k], dst_ref=parts.at[other, k],
            send_sem=y_send.at[j, k], recv_sem=y_recv.at[other, k],
            device_id=(me, other), device_id_type=MESH,
        )

    tokens_by = lax.broadcasted_iota(jnp.int32, (tok_count, tok_count), 0)
    earlier = tokens_by < lax.broadcasted_iota(jnp.int32, (tok_count, tok_count), 1)
    experts = lax.broadcasted_iota(jnp.int32, (round_up(n, 16), tok_count), 0)
    named = [experts == routes_ref[j : j + 1, :] for j in range(2)]
    before = jnp.dot(
        jnp.where(named[0] | named[1], 1.0, 0.0).astype(BF16),
        jnp.where(earlier, 1.0, 0.0).astype(BF16),
        preferred_element_type=F32,
    )
    for j in range(2):
        rank = jnp.sum(jnp.where(named[j], before, 0.0), axis=0, keepdims=True)
        slots_ref[j : j + 1, :] = routes_ref[j : j + 1, :] * cap + rank.astype(jnp.int32)

    def build(k, msg_to, p_to):
        dest = towards(k)[0]
        probs = prob_ref[...].astype(F32)
        place = lax.broadcasted_iota(jnp.int32, (pair, tok_count), 0)
        first = slots_ref[0:1, :] - dest * cap
        second = slots_ref[1:2, :] - dest * cap
        is_x = place < cap
        is_dy = (place >= cap) & (place < 2 * cap)
        pick_x = is_x & ((first == place) | (second == place))
        pick_dy = is_dy & ((first + cap == place) | (second + cap == place))
        picked = jnp.dot(
            jnp.where(pick_x, 1.0, 0.0).astype(BF16), tok_ref[...], preferred_element_type=F32
        ) + jnp.dot(
            jnp.where(pick_dy, 1.0, 0.0).astype(BF16), dy_ref[...], preferred_element_type=F32
        )
        msg_to[k] = picked.astype(BF16)
        spot = lax.broadcasted_iota(jnp.int32, (rows, tok_count), 0)
        prob = jnp.where(first == spot, probs[0:1, :], 0.0) + jnp.where(
            second == spot, probs[1:2, :], 0.0
        )
        p_to[k] = jnp.broadcast_to(
            to_row(jnp.sum(prob, axis=1, keepdims=True)), p_to.shape[1:]
        )

    def start(q):
        p_copy(q).start()
        msg_copy(q).start()

    build(1, msg, p_out)
    start(1)
    for q in range(3, 2 * ahead, 2):
        build(q, msg, p_out)
        start(q)
    for q in range(2, 2 * ahead, 2):
        build(q, msg, p_out)
        start(q)
    build(0, recv, p_in)
    for i in range(3):
        w_copy(i).wait()

    def project(k):
        both = lax.dot_general(
            recv[k], w_all[...], (((1,), (1,)), ((), ())), preferred_element_type=F32
        )
        parts[mine, k, :, 0 : 2 * hid] = both[0:rows, 0 : 2 * hid]
        parts[mine, k, :, 2 * hid : 3 * hid] = pltpu.roll(
            both[:, 2 * hid : 3 * hid], pair - cap, 0
        )[0:rows]
        for j in range(1, dp):
            y_copy(j, k).start()

    def combine_rows(k):
        for j in range(1, dp):
            y_arrival(j, k).wait_recv()
        total = parts[0, k]
        for r in range(1, dp):
            total = total + parts[r, k]
        gate_pre = total[:, 0:hid]
        up_pre = total[:, hid : 2 * hid]
        grad_hid = total[:, 2 * hid : 3 * hid]
        real = lax.broadcasted_iota(jnp.int32, (rows, hid), 0) < cap
        weight = to_col(p_in[k][0:1, :], rows)
        sig = jax.nn.sigmoid(gate_pre)
        silu_out = gate_pre * sig
        slope = sig * (1.0 + gate_pre * (1.0 - sig))
        hidden = silu_out * up_pre
        scaled = weight * grad_hid
        scores = jnp.sum(jnp.where(real, hidden * grad_hid, 0.0), axis=1, keepdims=True)

        def spread(value):
            value = jnp.where(real, value, 0.0)
            return jnp.concatenate([value, jnp.zeros((pair - rows, hid), F32)], axis=0)

        rows_a[k, :, 0:hid] = spread(scaled * up_pre * slope).astype(BF16)
        rows_a[k, :, hid : 2 * hid] = spread(scaled * silu_out).astype(BF16)
        rows_a[k, :, 2 * hid : 3 * hid] = pltpu.roll(
            spread(weight * hidden), cap, 0
        ).astype(BF16)
        return jnp.broadcast_to(to_row(scores), s_out.shape[1:])

    def finish(q):
        p_copy(q).wait_recv()
        s_out[q] = combine_rows(q)
        s_copy(q).start()

    def step(i, first=False):
        near, far = 2 * i, 2 * i + 1
        later = 2 * (i + ahead)
        msg_copy(near).wait_recv()
        project(near)
        if first:
            s_in[0] = combine_rows(0)
        else:
            finish(near - 2)
        finish(far - 2)

        @pl.when(i + ahead < half)
        def _():
            build(later + 1, msg, p_out)
            build(later, msg, p_out)

        msg_copy(far).wait_recv()

        @pl.when(i + ahead < half)
        def _():
            msg_copy(far).wait_send()
            start(later + 1)
            start(later)

        project(far)

    def out_copy(j, c):
        at = pl.ds(pl.multiple_of(c * tile, tile), tile)
        return pltpu.make_async_copy(
            staged.at[j, :, at], (gate_ref, up_ref, down_ref)[j].at[0, :, at], o_sem.at[j, c]
        )

    def outer(lo, hi, opening, closing):
        depth = (hi - lo) * pair

        def columns(c, _):
            at = pl.ds(pl.multiple_of(c * tile, tile), tile)
            new = lax.dot_general(
                rows_a[lo:hi].reshape(depth, 3 * hid), recv[lo:hi, :, at].reshape(depth, tile),
                (((0,), (0,)), ((), ())), preferred_element_type=F32,
            )
            if not opening:
                new = new + acc[:, at]
            if closing:
                for j in range(3):
                    staged[j, :, at] = new[j * hid : (j + 1) * hid].astype(BF16)
                    out_copy(j, c).start()
            else:
                acc[:, at] = new
            return 0

        lax.fori_loop(0, width // tile, columns, 0)

    project(0)
    build(2 * ahead + 1, msg, p_out)
    build(2 * ahead, msg, p_out)
    msg_copy(1).wait_recv()
    msg_copy(1).wait_send()
    start(2 * ahead + 1)
    start(2 * ahead)
    project(1)
    step(1, first=True)

    def steps(i, _):
        step(i)
        return 0

    lax.fori_loop(2, half // 2 + 1, steps, 0)
    outer(0, half, True, False)
    lax.fori_loop(half // 2 + 1, half - 1, steps, 0)
    msg_copy(n - 2).wait_recv()
    project(n - 2)
    finish(n - 4)
    outer(half, n - 3, False, False)
    finish(n - 3)
    msg_copy(n - 1).wait_recv()
    project(n - 1)
    finish(n - 2)
    finish(n - 1)
    outer(n - 3, n, False, True)

    def gather_scores(k, carry):
        one, two = carry
        spot = lax.broadcasted_iota(jnp.int32, (rows, tok_count), 0)
        spot = jnp.where(spot < cap, spot + towards(k)[0] * cap, -1)
        col = to_col(s_in[k][0:1, :], rows)
        one = one + jnp.sum(jnp.where(slots_ref[0:1, :] == spot, col, 0.0), axis=0, keepdims=True)
        two = two + jnp.sum(jnp.where(slots_ref[1:2, :] == spot, col, 0.0), axis=0, keepdims=True)
        return one, two

    def arrived(k, carry):
        s_copy(k).wait_recv()
        return gather_scores(k, carry)

    zero = jnp.zeros((1, tok_count), F32)
    one, two = lax.fori_loop(1, n, arrived, gather_scores(0, (zero, zero)))
    comb_ref[0:1, :] = one
    comb_ref[1:2, :] = two

    def drain(q, _):
        p_copy(q).wait_send()
        s_copy(q).wait_send()
        return 0

    def drain_near(i, _):
        msg_copy(2 * i).wait_send()
        return 0

    lax.fori_loop(1, n, drain, 0)
    lax.fori_loop(1, half, drain_near, 0)
    for i in range(half - ahead, half):
        msg_copy(2 * i + 1).wait_send()

    def drain_parts(k, _):
        for j in range(1, dp):
            y_copy(j, k).wait_send()
        return 0

    lax.fori_loop(0, n, drain_parts, 0)

    def drain_out(c, _):
        for j in range(3):
            out_copy(j, c).wait()
        return 0

    lax.fori_loop(0, width // tile, drain_out, 0)


def local(n, dp, tokens, grad_out, combine, routes, w_gate, w_up, w_down):
    tok_count, width = tokens.shape
    hid = w_gate.shape[1]
    top_count = routes.shape[1]
    cap = max(2, (9 * tok_count * top_count + 8 * n - 1) // (8 * n))
    pair = round_up(2 * cap, 8)
    rows = round_up(cap, 8)
    tile = 512 if width % 512 == 0 else 256
    grad_shape = jax.ShapeDtypeStruct((1, hid, width), BF16)
    vmem = pl.BlockSpec(memory_space=pltpu.VMEM)
    hbm = pl.BlockSpec(memory_space=pl.ANY)
    dma = pltpu.SemaphoreType.DMA
    gate, up, down, comb = pl.pallas_call(
        functools.partial(kernel, n, dp, cap, tile, 2),
        out_shape=(
            grad_shape, grad_shape, grad_shape,
            jax.ShapeDtypeStruct((top_count, tok_count), F32),
        ),
        in_specs=[vmem] * 4 + [hbm] * 3,
        out_specs=(hbm, hbm, hbm, vmem),
        scratch_shapes=[
            pltpu.VMEM((top_count, tok_count), jnp.int32),
            pltpu.VMEM((n, pair, width), BF16),
            pltpu.VMEM((n, pair, width), BF16),
            pltpu.VMEM((3, hid, width), BF16),
            pltpu.VMEM((3 * hid, width), BF16),
            pltpu.VMEM((n, pair, 3 * hid), BF16),
            pltpu.VMEM((3 * hid, width), F32),
            pltpu.VMEM((dp, n, rows, 3 * hid), F32),
            pltpu.VMEM((n, 8, 128), F32),
            pltpu.VMEM((n, 8, 128), F32),
            pltpu.VMEM((n, 8, 128), F32),
            pltpu.VMEM((n, 8, 128), F32),
            dma((3,)),
            dma((n,)), dma((n,)), dma((n,)), dma((n,)), dma((n,)), dma((n,)),
            dma((dp, n)), dma((dp, n)), dma((3, width // tile)),
        ],
        compiler_params=pltpu.CompilerParams(
            collective_id=0, has_side_effects=True, vmem_limit_bytes=60 * 1024 * 1024
        ),
        cost_estimate=pl.CostEstimate(
            flops=12 * n * cap * hid * width, bytes_accessed=20 * hid * width, transcendentals=0
        ),
    )(routes.T, combine.T, tokens, grad_out, w_gate, w_up, w_down)
    return gate, up, down, comb.T


def solution(mesh):
    placed = (
        P("expert", "dp"),
        P("expert", "dp"),
        P("expert", None),
        P("expert", None),
        P("expert", None, "dp"),
        P("expert", None, "dp"),
        P("expert", None, "dp"),
    )
    return jax.shard_map(
        functools.partial(local, mesh.shape["expert"], mesh.shape["dp"]),
        mesh=mesh,
        in_specs=placed,
        out_specs=(
            P("expert", None, "dp"),
            P("expert", None, "dp"),
            P("expert", None, "dp"),
            P("expert", None),
        ),
        check_vma=False,
    )
```

```python
import functools

import jax
import jax.numpy as jnp
from jax import lax
from jax.experimental import pallas as pl
from jax.experimental.pallas import tpu as pltpu
from jax.sharding import PartitionSpec as P

MESH = pl.DeviceIdType.MESH
F32 = jnp.float32
BF16 = jnp.bfloat16


def round_up(value, unit):
    return (value + unit - 1) // unit * unit


def partner_of(me, k, n):
    out, bit = 0, 1
    while bit < n:
        out = out + (me // bit + k // bit) % 2 * bit
        bit *= 2
    return out


def diagonal(rows):
    return lax.broadcasted_iota(jnp.int32, (rows, 128), 0) == lax.broadcasted_iota(
        jnp.int32, (rows, 128), 1
    )


def to_row(col):
    rows = col.shape[0]
    return jnp.sum(jnp.where(diagonal(rows), col, 0.0), axis=0, keepdims=True)


def to_col(row, rows):
    return jnp.sum(jnp.where(diagonal(rows), row, 0.0), axis=1, keepdims=True)


def kernel(
    n, dp, cap, tile, groups,
    routes_ref, prob_ref, tok_ref, dy_ref, wg_ref, wu_ref, wd_ref,
    gate_ref, up_ref, down_ref, comb_ref,
    slots_ref, msg, recv, staged, w_all, rows_a, acc, parts, p_out, p_in, s_out, s_in,
    w_sem, m_send, m_recv, p_send, p_recv, s_send, s_recv, y_send, y_recv, o_sem,
):
    me = lax.axis_index("expert")
    mine = lax.axis_index("dp")
    tok_count, width = tok_ref.shape
    hid = wg_ref.shape[1]
    pair = msg.shape[1]
    rows = parts.shape[2]
    half = n // 2

    def towards(k):
        return (partner_of(me, k, n), mine)

    def w_copy(i):
        src = (wg_ref, wu_ref, wd_ref)[i]
        return pltpu.make_async_copy(src.at[0], staged.at[i], w_sem.at[i])

    for i in range(3):
        w_copy(i).start()

    barrier = pltpu.get_barrier_semaphore()

    def greet(k, _):
        pl.semaphore_signal(
            barrier, inc=1, device_id=(partner_of(me, k, n), mine), device_id_type=MESH
        )
        return 0

    lax.fori_loop(1, n, greet, 0)
    for j in range(1, dp):
        pl.semaphore_signal(
            barrier, inc=1, device_id=(me, (mine + j) % dp), device_id_type=MESH
        )
    pl.semaphore_wait(barrier, n - 1 + dp - 1)

    def msg_copy(q):
        return pltpu.make_async_remote_copy(
            src_ref=msg.at[q], dst_ref=recv.at[q], send_sem=m_send.at[q], recv_sem=m_recv.at[q],
            device_id=towards(q), device_id_type=MESH,
        )

    def p_copy(q):
        return pltpu.make_async_remote_copy(
            src_ref=p_out.at[q], dst_ref=p_in.at[q], send_sem=p_send.at[q], recv_sem=p_recv.at[q],
            device_id=towards(q), device_id_type=MESH,
        )

    def s_copy(q):
        return pltpu.make_async_remote_copy(
            src_ref=s_out.at[q], dst_ref=s_in.at[q], send_sem=s_send.at[q], recv_sem=s_recv.at[q],
            device_id=towards(q), device_id_type=MESH,
        )

    def y_copy(j, k):
        return pltpu.make_async_remote_copy(
            src_ref=parts.at[mine, k], dst_ref=parts.at[mine, k],
            send_sem=y_send.at[j, k], recv_sem=y_recv.at[mine, k],
            device_id=(me, (mine + j) % dp), device_id_type=MESH,
        )

    def y_arrival(j, k):
        other = (mine + j) % dp
        return pltpu.make_async_remote_copy(
            src_ref=parts.at[other, k], dst_ref=parts.at[other, k],
            send_sem=y_send.at[j, k], recv_sem=y_recv.at[other, k],
            device_id=(me, other), device_id_type=MESH,
        )

    tokens_by = lax.broadcasted_iota(jnp.int32, (tok_count, tok_count), 0)
    earlier = tokens_by < lax.broadcasted_iota(jnp.int32, (tok_count, tok_count), 1)
    experts = lax.broadcasted_iota(jnp.int32, (round_up(n, 16), tok_count), 0)
    named = [experts == routes_ref[j : j + 1, :] for j in range(2)]
    before = jnp.dot(
        jnp.where(named[0] | named[1], 1.0, 0.0).astype(BF16),
        jnp.where(earlier, 1.0, 0.0).astype(BF16),
        preferred_element_type=F32,
    )
    for j in range(2):
        rank = jnp.sum(jnp.where(named[j], before, 0.0), axis=0, keepdims=True)
        slots_ref[j : j + 1, :] = routes_ref[j : j + 1, :] * cap + rank.astype(jnp.int32)

    def build(k, msg_to, p_to):
        dest = towards(k)[0]
        probs = prob_ref[...].astype(F32)
        place = lax.broadcasted_iota(jnp.int32, (pair, tok_count), 0)
        first = slots_ref[0:1, :] - dest * cap
        second = slots_ref[1:2, :] - dest * cap
        is_x = place < cap
        is_dy = (place >= cap) & (place < 2 * cap)
        pick_x = is_x & ((first == place) | (second == place))
        pick_dy = is_dy & ((first + cap == place) | (second + cap == place))
        picked = jnp.dot(
            jnp.where(pick_x, 1.0, 0.0).astype(BF16), tok_ref[...], preferred_element_type=F32
        ) + jnp.dot(
            jnp.where(pick_dy, 1.0, 0.0).astype(BF16), dy_ref[...], preferred_element_type=F32
        )
        msg_to[k] = picked.astype(BF16)
        spot = lax.broadcasted_iota(jnp.int32, (rows, tok_count), 0)
        prob = jnp.where(first == spot, probs[0:1, :], 0.0) + jnp.where(
            second == spot, probs[1:2, :], 0.0
        )
        p_to[k] = jnp.broadcast_to(
            to_row(jnp.sum(prob, axis=1, keepdims=True)), p_to.shape[1:]
        )

    def start(q):
        p_copy(q).start()
        msg_copy(q).start()

    def send(i, _):
        k = (half + i) % n + i // half
        build(k, msg, p_out)
        start(k)
        return 0

    lax.fori_loop(0, n - 1, send, 0)
    build(0, recv, p_in)
    for i in range(3):
        w_copy(i).wait()

    def turn(c, _):
        at = pl.ds(pl.multiple_of(c * tile, tile), tile)
        for i in range(3):
            w_all[at, i * hid : (i + 1) * hid] = staged[i, :, at].T
        return 0

    lax.fori_loop(0, width // tile, turn, 0)

    def project(k):
        both = lax.dot_general(
            recv[k], w_all[...], (((1,), (0,)), ((), ())), preferred_element_type=F32
        )
        parts[mine, k, :, 0 : 2 * hid] = both[0:rows, 0 : 2 * hid]
        parts[mine, k, :, 2 * hid : 3 * hid] = pltpu.roll(
            both[:, 2 * hid : 3 * hid], pair - cap, 0
        )[0:rows]
        for j in range(1, dp):
            y_copy(j, k).start()

    def combine_rows(k):
        for j in range(1, dp):
            y_arrival(j, k).wait_recv()
        total = parts[0, k]
        for r in range(1, dp):
            total = total + parts[r, k]
        gate_pre = total[:, 0:hid]
        up_pre = total[:, hid : 2 * hid]
        grad_hid = total[:, 2 * hid : 3 * hid]
        real = lax.broadcasted_iota(jnp.int32, (rows, hid), 0) < cap
        weight = to_col(p_in[k][0:1, :], rows)
        sig = jax.nn.sigmoid(gate_pre)
        silu_out = gate_pre * sig
        slope = sig * (1.0 + gate_pre * (1.0 - sig))
        hidden = silu_out * up_pre
        scaled = weight * grad_hid
        scores = jnp.sum(jnp.where(real, hidden * grad_hid, 0.0), axis=1, keepdims=True)

        def spread(value):
            value = jnp.where(real, value, 0.0)
            return jnp.concatenate([value, jnp.zeros((pair - rows, hid), F32)], axis=0)

        rows_a[k, :, 0:hid] = spread(scaled * up_pre * slope).astype(BF16)
        rows_a[k, :, hid : 2 * hid] = spread(scaled * silu_out).astype(BF16)
        rows_a[k, :, 2 * hid : 3 * hid] = pltpu.roll(
            spread(weight * hidden), cap, 0
        ).astype(BF16)
        return jnp.broadcast_to(to_row(scores), s_out.shape[1:])

    def finish(q):
        p_copy(q).wait_recv()
        s_out[q] = combine_rows(q)
        s_copy(q).start()

    def step(k, _):
        msg_copy(k).wait_recv()
        project(k)
        finish(k - 1)
        return 0

    def out_copy(j, c):
        at = pl.ds(pl.multiple_of(c * tile, tile), tile)
        return pltpu.make_async_copy(
            staged.at[j, :, at], (gate_ref, up_ref, down_ref)[j].at[0, :, at], o_sem.at[j, c]
        )

    def outer(lo, hi, opening, closing):
        depth = (hi - lo) * pair
        turned = rows_a[lo:hi].reshape(depth, 3 * hid).T

        def columns(c, _):
            at = pl.ds(pl.multiple_of(c * tile, tile), tile)
            new = jnp.dot(
                turned, recv[lo:hi, :, at].reshape(depth, tile), preferred_element_type=F32
            )
            if not opening:
                new = new + acc[:, at]
            if closing:
                for j in range(3):
                    staged[j, :, at] = new[j * hid : (j + 1) * hid].astype(BF16)
                    out_copy(j, c).start()
            else:
                acc[:, at] = new
            return 0

        lax.fori_loop(0, width // tile, columns, 0)

    project(0)
    msg_copy(1).wait_recv()
    project(1)
    s_in[0] = combine_rows(0)
    done, k = 0, 2
    for bound in groups:
        lax.fori_loop(k, min(bound + 1, n), step, 0)
        k = min(bound + 1, n)
        if bound == n:
            finish(n - 1)
        outer(done, bound, done == 0, bound == n)
        done = bound

    def gather_scores(k, carry):
        one, two = carry
        spot = lax.broadcasted_iota(jnp.int32, (rows, tok_count), 0)
        spot = jnp.where(spot < cap, spot + towards(k)[0] * cap, -1)
        col = to_col(s_in[k][0:1, :], rows)
        one = one + jnp.sum(jnp.where(slots_ref[0:1, :] == spot, col, 0.0), axis=0, keepdims=True)
        two = two + jnp.sum(jnp.where(slots_ref[1:2, :] == spot, col, 0.0), axis=0, keepdims=True)
        return one, two

    def arrived(k, carry):
        s_copy(k).wait_recv()
        return gather_scores(k, carry)

    zero = jnp.zeros((1, tok_count), F32)
    one, two = lax.fori_loop(1, n, arrived, gather_scores(0, (zero, zero)))
    comb_ref[0:1, :] = one
    comb_ref[1:2, :] = two

    def drain(k, _):
        msg_copy(k).wait_send()
        p_copy(k).wait_send()
        s_copy(k).wait_send()
        return 0

    lax.fori_loop(1, n, drain, 0)

    def drain_parts(k, _):
        for j in range(1, dp):
            y_copy(j, k).wait_send()
        return 0

    lax.fori_loop(0, n, drain_parts, 0)

    def drain_out(c, _):
        for j in range(3):
            out_copy(j, c).wait()
        return 0

    lax.fori_loop(0, width // tile, drain_out, 0)


def local(n, dp, tokens, grad_out, combine, routes, w_gate, w_up, w_down):
    tok_count, width = tokens.shape
    hid = w_gate.shape[1]
    top_count = routes.shape[1]
    cap = max(2, (9 * tok_count * top_count + 8 * n - 1) // (8 * n))
    pair = round_up(2 * cap, 8)
    rows = round_up(cap, 8)
    tile = 512 if width % 512 == 0 else 256
    grad_shape = jax.ShapeDtypeStruct((1, hid, width), BF16)
    vmem = pl.BlockSpec(memory_space=pltpu.VMEM)
    hbm = pl.BlockSpec(memory_space=pl.ANY)
    dma = pltpu.SemaphoreType.DMA
    gate, up, down, comb = pl.pallas_call(
        functools.partial(kernel, n, dp, cap, tile, (n // 2, n - 3, n)),
        out_shape=(
            grad_shape, grad_shape, grad_shape,
            jax.ShapeDtypeStruct((top_count, tok_count), F32),
        ),
        in_specs=[vmem] * 4 + [hbm] * 3,
        out_specs=(hbm, hbm, hbm, vmem),
        scratch_shapes=[
            pltpu.VMEM((top_count, tok_count), jnp.int32),
            pltpu.VMEM((n, pair, width), BF16),
            pltpu.VMEM((n, pair, width), BF16),
            pltpu.VMEM((3, hid, width), BF16),
            pltpu.VMEM((width, 3 * hid), BF16),
            pltpu.VMEM((n, pair, 3 * hid), BF16),
            pltpu.VMEM((3 * hid, width), F32),
            pltpu.VMEM((dp, n, rows, 3 * hid), F32),
            pltpu.VMEM((n, 8, 128), F32),
            pltpu.VMEM((n, 8, 128), F32),
            pltpu.VMEM((n, 8, 128), F32),
            pltpu.VMEM((n, 8, 128), F32),
            dma((3,)),
            dma((n,)), dma((n,)), dma((n,)), dma((n,)), dma((n,)), dma((n,)),
            dma((dp, n)), dma((dp, n)), dma((3, width // tile)),
        ],
        compiler_params=pltpu.CompilerParams(
            collective_id=0, has_side_effects=True, vmem_limit_bytes=47 * 1024 * 1024
        ),
        cost_estimate=pl.CostEstimate(
            flops=12 * n * cap * hid * width, bytes_accessed=20 * hid * width, transcendentals=0
        ),
    )(routes.T, combine.T, tokens, grad_out, w_gate, w_up, w_down)
    return gate, up, down, comb.T


def solution(mesh):
    placed = (
        P("expert", "dp"),
        P("expert", "dp"),
        P("expert", None),
        P("expert", None),
        P("expert", None, "dp"),
        P("expert", None, "dp"),
        P("expert", None, "dp"),
    )
    return jax.shard_map(
        functools.partial(local, mesh.shape["expert"], mesh.shape["dp"]),
        mesh=mesh,
        in_specs=placed,
        out_specs=(
            P("expert", None, "dp"),
            P("expert", None, "dp"),
            P("expert", None, "dp"),
            P("expert", None),
        ),
        check_vma=False,
    )
```

```python
import functools

import jax
import jax.numpy as jnp
from jax import lax
from jax.experimental import pallas as pl
from jax.experimental.pallas import tpu as pltpu
from jax.sharding import PartitionSpec as P

MESH = pl.DeviceIdType.MESH
F32 = jnp.float32
BF16 = jnp.bfloat16


def round_up(value, unit):
    return (value + unit - 1) // unit * unit


def partner_of(me, k, n):
    out, bit = 0, 1
    while bit < n:
        out = out + (me // bit + k // bit) % 2 * bit
        bit *= 2
    return out


def diagonal(rows):
    return lax.broadcasted_iota(jnp.int32, (rows, 128), 0) == lax.broadcasted_iota(
        jnp.int32, (rows, 128), 1
    )


def to_row(col):
    rows = col.shape[0]
    return jnp.sum(jnp.where(diagonal(rows), col, 0.0), axis=0, keepdims=True)


def to_col(row, rows):
    return jnp.sum(jnp.where(diagonal(rows), row, 0.0), axis=1, keepdims=True)


def kernel(
    n, dp, cap, tile, groups,
    routes_ref, prob_ref, tok_ref, dy_ref, wg_ref, wu_ref, wd_ref,
    gate_ref, up_ref, down_ref, comb_ref,
    slots_ref, msg, recv, staged, w_all, rows_a, acc, parts, p_out, p_in, s_out, s_in,
    w_sem, m_send, m_recv, p_send, p_recv, s_send, s_recv, y_send, y_recv, o_sem,
):
    me = lax.axis_index("expert")
    mine = lax.axis_index("dp")
    tok_count, width = tok_ref.shape
    hid = wg_ref.shape[1]
    pair = msg.shape[1]
    rows = parts.shape[2] // 2
    half = n // 2

    def towards(k):
        return (partner_of(me, k, n), mine)

    def w_copy(i):
        src = (wg_ref, wu_ref, wd_ref)[i]
        return pltpu.make_async_copy(src.at[0], staged.at[i], w_sem.at[i])

    for i in range(3):
        w_copy(i).start()

    barrier = pltpu.get_barrier_semaphore()

    def greet(k, _):
        pl.semaphore_signal(
            barrier, inc=1, device_id=(partner_of(me, k, n), mine), device_id_type=MESH
        )
        return 0

    lax.fori_loop(1, n, greet, 0)
    for j in range(1, dp):
        pl.semaphore_signal(
            barrier, inc=1, device_id=(me, (mine + j) % dp), device_id_type=MESH
        )
    pl.semaphore_wait(barrier, n - 1 + dp - 1)

    def msg_copy(q):
        return pltpu.make_async_remote_copy(
            src_ref=msg.at[q], dst_ref=recv.at[q], send_sem=m_send.at[q], recv_sem=m_recv.at[q],
            device_id=towards(q), device_id_type=MESH,
        )

    def p_copy(q):
        return pltpu.make_async_remote_copy(
            src_ref=p_out.at[q], dst_ref=p_in.at[q], send_sem=p_send.at[q], recv_sem=p_recv.at[q],
            device_id=towards(q), device_id_type=MESH,
        )

    def s_copy(q):
        return pltpu.make_async_remote_copy(
            src_ref=s_out.at[q], dst_ref=s_in.at[q], send_sem=s_send.at[q], recv_sem=s_recv.at[q],
            device_id=towards(q), device_id_type=MESH,
        )

    def y_copy(j, k):
        return pltpu.make_async_remote_copy(
            src_ref=parts.at[mine, k], dst_ref=parts.at[mine, k],
            send_sem=y_send.at[j, k], recv_sem=y_recv.at[mine, k],
            device_id=(me, (mine + j) % dp), device_id_type=MESH,
        )

    def y_arrival(j, k):
        other = (mine + j) % dp
        return pltpu.make_async_remote_copy(
            src_ref=parts.at[other, k], dst_ref=parts.at[other, k],
            send_sem=y_send.at[j, k], recv_sem=y_recv.at[other, k],
            device_id=(me, other), device_id_type=MESH,
        )

    tokens_by = lax.broadcasted_iota(jnp.int32, (tok_count, tok_count), 0)
    earlier = tokens_by < lax.broadcasted_iota(jnp.int32, (tok_count, tok_count), 1)
    experts = lax.broadcasted_iota(jnp.int32, (round_up(n, 16), tok_count), 0)
    named = [experts == routes_ref[j : j + 1, :] for j in range(2)]
    before = jnp.dot(
        jnp.where(named[0] | named[1], 1.0, 0.0).astype(BF16),
        jnp.where(earlier, 1.0, 0.0).astype(BF16),
        preferred_element_type=F32,
    )
    for j in range(2):
        rank = jnp.sum(jnp.where(named[j], before, 0.0), axis=0, keepdims=True)
        slots_ref[j : j + 1, :] = routes_ref[j : j + 1, :] * cap + rank.astype(jnp.int32)

    def build(k, msg_to, p_to):
        dest = towards(k)[0]
        probs = prob_ref[...].astype(F32)
        place = lax.broadcasted_iota(jnp.int32, (pair, tok_count), 0)
        first = slots_ref[0:1, :] - dest * cap
        second = slots_ref[1:2, :] - dest * cap
        is_x = place < cap
        is_dy = (place >= cap) & (place < 2 * cap)
        pick_x = is_x & ((first == place) | (second == place))
        pick_dy = is_dy & ((first + cap == place) | (second + cap == place))
        picked = jnp.dot(
            jnp.where(pick_x, 1.0, 0.0).astype(BF16), tok_ref[...], preferred_element_type=F32
        ) + jnp.dot(
            jnp.where(pick_dy, 1.0, 0.0).astype(BF16), dy_ref[...], preferred_element_type=F32
        )
        msg_to[k] = picked.astype(BF16)
        spot = lax.broadcasted_iota(jnp.int32, (rows, tok_count), 0)
        prob = jnp.where(first == spot, probs[0:1, :], 0.0) + jnp.where(
            second == spot, probs[1:2, :], 0.0
        )
        p_to[k] = jnp.broadcast_to(
            to_row(jnp.sum(prob, axis=1, keepdims=True)), p_to.shape[1:]
        )

    def start(q):
        p_copy(q).start()
        msg_copy(q).start()

    def send(i, _):
        k = (half + i) % n + i // half
        build(k, msg, p_out)
        start(k)
        return 0

    lax.fori_loop(0, n - 1, send, 0)
    build(0, recv, p_in)
    for i in range(3):
        w_copy(i).wait()

    def turn(c, _):
        at = pl.ds(pl.multiple_of(c * tile, tile), tile)
        for i in range(3):
            w_all[at, i * hid : (i + 1) * hid] = staged[i, :, at].T
        return 0

    lax.fori_loop(0, width // tile, turn, 0)

    def project(j):
        both = jnp.dot(
            recv[pl.ds(2 * j, 2)].reshape(2 * pair, width), w_all[...], preferred_element_type=F32
        )
        held = []
        for b in range(2):
            block = both[b * pair : (b + 1) * pair]
            moved = pltpu.roll(block[:, 2 * hid : 3 * hid], pair - cap, 0)
            held.append(jnp.concatenate([block[0:rows, 0 : 2 * hid], moved[0:rows]], axis=1))
        parts[mine, j] = jnp.concatenate(held, axis=0).astype(BF16)
        for other in range(1, dp):
            y_copy(other, j).start()

    def combine_rows(j):
        for other in range(1, dp):
            y_arrival(other, j).wait_recv()
        total = parts[0, j].astype(F32)
        for r in range(1, dp):
            total = total + parts[r, j].astype(F32)
        gate_pre = total[:, 0:hid]
        up_pre = total[:, hid : 2 * hid]
        grad_hid = total[:, 2 * hid : 3 * hid]
        real = lax.broadcasted_iota(jnp.int32, (rows, hid), 0) < cap
        weight = jnp.concatenate(
            [to_col(p_in[2 * j][0:1, :], rows), to_col(p_in[2 * j + 1][0:1, :], rows)], axis=0
        )
        sig = jax.nn.sigmoid(gate_pre)
        silu_out = gate_pre * sig
        slope = sig * (1.0 + gate_pre * (1.0 - sig))
        hidden = silu_out * up_pre
        scaled = weight * grad_hid
        products = hidden * grad_hid
        scores = []
        for b in range(2):
            here = slice(b * rows, (b + 1) * rows)

            def spread(value):
                value = jnp.where(real, value[here], 0.0)
                return jnp.concatenate([value, jnp.zeros((pair - rows, hid), F32)], axis=0)

            k = 2 * j + b
            rows_a[k, :, 0:hid] = spread(scaled * up_pre * slope).astype(BF16)
            rows_a[k, :, hid : 2 * hid] = spread(scaled * silu_out).astype(BF16)
            rows_a[k, :, 2 * hid : 3 * hid] = pltpu.roll(
                spread(weight * hidden), cap, 0
            ).astype(BF16)
            col = jnp.sum(jnp.where(real, products[here], 0.0), axis=1, keepdims=True)
            scores.append(jnp.broadcast_to(to_row(col), s_out.shape[1:]))
        return scores

    def finish(j):
        p_copy(2 * j).wait_recv()
        p_copy(2 * j + 1).wait_recv()
        scores = combine_rows(j)
        for b in range(2):
            s_out[2 * j + b] = scores[b]
            s_copy(2 * j + b).start()

    def step(j, _):
        msg_copy(2 * j).wait_recv()
        msg_copy(2 * j + 1).wait_recv()
        project(j)
        finish(j - 1)
        return 0

    def out_copy(j, c):
        at = pl.ds(pl.multiple_of(c * tile, tile), tile)
        return pltpu.make_async_copy(
            staged.at[j, :, at], (gate_ref, up_ref, down_ref)[j].at[0, :, at], o_sem.at[j, c]
        )

    def outer(lo, hi, opening, closing):
        depth = (hi - lo) * pair
        turned = rows_a[lo:hi].reshape(depth, 3 * hid).T

        def columns(c, _):
            at = pl.ds(pl.multiple_of(c * tile, tile), tile)
            new = jnp.dot(
                turned, recv[lo:hi, :, at].reshape(depth, tile), preferred_element_type=F32
            )
            if not opening:
                new = new + acc[:, at]
            if closing:
                for j in range(3):
                    staged[j, :, at] = new[j * hid : (j + 1) * hid].astype(BF16)
                    out_copy(j, c).start()
            else:
                acc[:, at] = new
            return 0

        lax.fori_loop(0, width // tile, columns, 0)

    msg_copy(1).wait_recv()
    project(0)
    msg_copy(2).wait_recv()
    msg_copy(3).wait_recv()
    project(1)
    p_copy(1).wait_recv()
    scores = combine_rows(0)
    s_in[0] = scores[0]
    s_out[1] = scores[1]
    s_copy(1).start()
    done, j = 0, 2
    for bound in groups:
        upto = min(bound // 2 + 1, half)
        lax.fori_loop(j, upto, step, 0)
        j = upto
        if bound == n:
            finish(half - 1)
        outer(done, bound, done == 0, bound == n)
        done = bound

    def gather_scores(k, carry):
        one, two = carry
        spot = lax.broadcasted_iota(jnp.int32, (rows, tok_count), 0)
        spot = jnp.where(spot < cap, spot + towards(k)[0] * cap, -1)
        col = to_col(s_in[k][0:1, :], rows)
        one = one + jnp.sum(jnp.where(slots_ref[0:1, :] == spot, col, 0.0), axis=0, keepdims=True)
        two = two + jnp.sum(jnp.where(slots_ref[1:2, :] == spot, col, 0.0), axis=0, keepdims=True)
        return one, two

    def arrived(k, carry):
        s_copy(k).wait_recv()
        return gather_scores(k, carry)

    zero = jnp.zeros((1, tok_count), F32)
    one, two = lax.fori_loop(1, n, arrived, gather_scores(0, (zero, zero)))
    comb_ref[0:1, :] = one
    comb_ref[1:2, :] = two

    def drain(k, _):
        msg_copy(k).wait_send()
        p_copy(k).wait_send()
        s_copy(k).wait_send()
        return 0

    lax.fori_loop(1, n, drain, 0)

    def drain_parts(j, _):
        for other in range(1, dp):
            y_copy(other, j).wait_send()
        return 0

    lax.fori_loop(0, half, drain_parts, 0)

    def drain_out(c, _):
        for j in range(3):
            out_copy(j, c).wait()
        return 0

    lax.fori_loop(0, width // tile, drain_out, 0)


def local(n, dp, tokens, grad_out, combine, routes, w_gate, w_up, w_down):
    tok_count, width = tokens.shape
    hid = w_gate.shape[1]
    top_count = routes.shape[1]
    cap = max(2, (9 * tok_count * top_count + 8 * n - 1) // (8 * n))
    pair = round_up(2 * cap, 8)
    rows = round_up(cap, 8)
    tile = 512 if width % 512 == 0 else 256
    grad_shape = jax.ShapeDtypeStruct((1, hid, width), BF16)
    vmem = pl.BlockSpec(memory_space=pltpu.VMEM)
    hbm = pl.BlockSpec(memory_space=pl.ANY)
    dma = pltpu.SemaphoreType.DMA
    gate, up, down, comb = pl.pallas_call(
        functools.partial(kernel, n, dp, cap, tile, (n // 2, n - 2, n)),
        out_shape=(
            grad_shape, grad_shape, grad_shape,
            jax.ShapeDtypeStruct((top_count, tok_count), F32),
        ),
        in_specs=[vmem] * 4 + [hbm] * 3,
        out_specs=(hbm, hbm, hbm, vmem),
        scratch_shapes=[
            pltpu.VMEM((top_count, tok_count), jnp.int32),
            pltpu.VMEM((n, pair, width), BF16),
            pltpu.VMEM((n, pair, width), BF16),
            pltpu.VMEM((3, hid, width), BF16),
            pltpu.VMEM((width, 3 * hid), BF16),
            pltpu.VMEM((n, pair, 3 * hid), BF16),
            pltpu.VMEM((3 * hid, width), F32),
            pltpu.VMEM((dp, n // 2, 2 * rows, 3 * hid), BF16),
            pltpu.VMEM((n, 8, 128), F32),
            pltpu.VMEM((n, 8, 128), F32),
            pltpu.VMEM((n, 8, 128), F32),
            pltpu.VMEM((n, 8, 128), F32),
            dma((3,)),
            dma((n,)), dma((n,)), dma((n,)), dma((n,)), dma((n,)), dma((n,)),
            dma((dp, n // 2)), dma((dp, n // 2)), dma((3, width // tile)),
        ],
        compiler_params=pltpu.CompilerParams(
            collective_id=0, has_side_effects=True, vmem_limit_bytes=47 * 1024 * 1024
        ),
        cost_estimate=pl.CostEstimate(
            flops=12 * n * cap * hid * width, bytes_accessed=20 * hid * width, transcendentals=0
        ),
    )(routes.T, combine.T, tokens, grad_out, w_gate, w_up, w_down)
    return gate, up, down, comb.T


def solution(mesh):
    placed = (
        P("expert", "dp"),
        P("expert", "dp"),
        P("expert", None),
        P("expert", None),
        P("expert", None, "dp"),
        P("expert", None, "dp"),
        P("expert", None, "dp"),
    )
    return jax.shard_map(
        functools.partial(local, mesh.shape["expert"], mesh.shape["dp"]),
        mesh=mesh,
        in_specs=placed,
        out_specs=(
            P("expert", None, "dp"),
            P("expert", None, "dp"),
            P("expert", None, "dp"),
            P("expert", None),
        ),
        check_vma=False,
    )
```

```python
import functools

import jax
import jax.numpy as jnp
from jax import lax
from jax.experimental import pallas as pl
from jax.experimental.pallas import tpu as pltpu
from jax.sharding import PartitionSpec as P

MESH = pl.DeviceIdType.MESH
F32 = jnp.float32
BF16 = jnp.bfloat16


def round_up(value, unit):
    return (value + unit - 1) // unit * unit


def partner_of(me, k, n):
    out, bit = 0, 1
    while bit < n:
        out = out + (me // bit + k // bit) % 2 * bit
        bit *= 2
    return out


def diagonal(rows):
    return lax.broadcasted_iota(jnp.int32, (rows, 128), 0) == lax.broadcasted_iota(
        jnp.int32, (rows, 128), 1
    )


def to_row(col):
    rows = col.shape[0]
    return jnp.sum(jnp.where(diagonal(rows), col, 0.0), axis=0, keepdims=True)


def to_col(row, rows):
    return jnp.sum(jnp.where(diagonal(rows), row, 0.0), axis=1, keepdims=True)


def kernel(
    n, dp, cap, tile, groups,
    routes_ref, prob_ref, tok_ref, dy_ref, wg_ref, wu_ref, wd_ref,
    gate_ref, up_ref, down_ref, comb_ref,
    slots_ref, msg, recv, staged, w_all, rows_a, acc, parts, p_out, p_in, s_out, s_in,
    w_sem, m_send, m_recv, p_send, p_recv, s_send, s_recv, y_send, y_recv, o_sem,
):
    me = lax.axis_index("expert")
    mine = lax.axis_index("dp")
    tok_count, width = tok_ref.shape
    hid = wg_ref.shape[1]
    pair = msg.shape[1]
    rows = parts.shape[2] // 2
    half = n // 2

    def towards(k):
        return (partner_of(me, k % 2 * half + k // 2, n), mine)

    def w_copy(i):
        src = (wg_ref, wu_ref, wd_ref)[i]
        return pltpu.make_async_copy(src.at[0], staged.at[i], w_sem.at[i])

    for i in range(3):
        w_copy(i).start()

    barrier = pltpu.get_barrier_semaphore()

    def greet(k, _):
        pl.semaphore_signal(
            barrier, inc=1, device_id=(partner_of(me, k, n), mine), device_id_type=MESH
        )
        return 0

    lax.fori_loop(1, n, greet, 0)
    for j in range(1, dp):
        pl.semaphore_signal(
            barrier, inc=1, device_id=(me, (mine + j) % dp), device_id_type=MESH
        )
    pl.semaphore_wait(barrier, n - 1 + dp - 1)

    def msg_copy(q):
        return pltpu.make_async_remote_copy(
            src_ref=msg.at[q], dst_ref=recv.at[q], send_sem=m_send.at[q], recv_sem=m_recv.at[q],
            device_id=towards(q), device_id_type=MESH,
        )

    def p_copy(q):
        return pltpu.make_async_remote_copy(
            src_ref=p_out.at[q], dst_ref=p_in.at[q], send_sem=p_send.at[q], recv_sem=p_recv.at[q],
            device_id=towards(q), device_id_type=MESH,
        )

    def s_copy(q):
        return pltpu.make_async_remote_copy(
            src_ref=s_out.at[q], dst_ref=s_in.at[q], send_sem=s_send.at[q], recv_sem=s_recv.at[q],
            device_id=towards(q), device_id_type=MESH,
        )

    def y_copy(j, k):
        return pltpu.make_async_remote_copy(
            src_ref=parts.at[mine, k], dst_ref=parts.at[mine, k],
            send_sem=y_send.at[j, k], recv_sem=y_recv.at[mine, k],
            device_id=(me, (mine + j) % dp), device_id_type=MESH,
        )

    def y_arrival(j, k):
        other = (mine + j) % dp
        return pltpu.make_async_remote_copy(
            src_ref=parts.at[other, k], dst_ref=parts.at[other, k],
            send_sem=y_send.at[j, k], recv_sem=y_recv.at[other, k],
            device_id=(me, other), device_id_type=MESH,
        )

    tokens_by = lax.broadcasted_iota(jnp.int32, (tok_count, tok_count), 0)
    earlier = tokens_by < lax.broadcasted_iota(jnp.int32, (tok_count, tok_count), 1)
    experts = lax.broadcasted_iota(jnp.int32, (round_up(n, 16), tok_count), 0)
    named = [experts == routes_ref[j : j + 1, :] for j in range(2)]
    before = jnp.dot(
        jnp.where(named[0] | named[1], 1.0, 0.0).astype(BF16),
        jnp.where(earlier, 1.0, 0.0).astype(BF16),
        preferred_element_type=F32,
    )
    for j in range(2):
        rank = jnp.sum(jnp.where(named[j], before, 0.0), axis=0, keepdims=True)
        slots_ref[j : j + 1, :] = routes_ref[j : j + 1, :] * cap + rank.astype(jnp.int32)

    def build(k, msg_to, p_to):
        dest = towards(k)[0]
        probs = prob_ref[...].astype(F32)
        place = lax.broadcasted_iota(jnp.int32, (pair, tok_count), 0)
        first = slots_ref[0:1, :] - dest * cap
        second = slots_ref[1:2, :] - dest * cap
        is_x = place < cap
        is_dy = (place >= cap) & (place < 2 * cap)
        pick_x = is_x & ((first == place) | (second == place))
        pick_dy = is_dy & ((first + cap == place) | (second + cap == place))
        picked = jnp.dot(
            jnp.where(pick_x, 1.0, 0.0).astype(BF16), tok_ref[...], preferred_element_type=F32
        ) + jnp.dot(
            jnp.where(pick_dy, 1.0, 0.0).astype(BF16), dy_ref[...], preferred_element_type=F32
        )
        msg_to[k] = picked.astype(BF16)
        spot = lax.broadcasted_iota(jnp.int32, (rows, tok_count), 0)
        prob = jnp.where(first == spot, probs[0:1, :], 0.0) + jnp.where(
            second == spot, probs[1:2, :], 0.0
        )
        p_to[k] = jnp.broadcast_to(
            to_row(jnp.sum(prob, axis=1, keepdims=True)), p_to.shape[1:]
        )

    def start(q):
        p_copy(q).start()
        msg_copy(q).start()

    def send(i, _):
        k = i + i % 2 * 2
        build(k, msg, p_out)
        start(k)
        return 0

    build(1, msg, p_out)
    start(1)
    lax.fori_loop(1, n - 1, send, 0)
    build(0, recv, p_in)
    for i in range(3):
        w_copy(i).wait()

    def turn(c, _):
        at = pl.ds(pl.multiple_of(c * tile, tile), tile)
        for i in range(3):
            w_all[at, i * hid : (i + 1) * hid] = staged[i, :, at].T
        return 0

    lax.fori_loop(0, width // tile, turn, 0)

    def project(j):
        both = jnp.dot(
            recv[pl.ds(2 * j, 2)].reshape(2 * pair, width), w_all[...], preferred_element_type=F32
        )
        held = []
        for b in range(2):
            block = both[b * pair : (b + 1) * pair]
            moved = pltpu.roll(block[:, 2 * hid : 3 * hid], pair - cap, 0)
            held.append(jnp.concatenate([block[0:rows, 0 : 2 * hid], moved[0:rows]], axis=1))
        parts[mine, j] = jnp.concatenate(held, axis=0)
        for other in range(1, dp):
            y_copy(other, j).start()

    def combine_rows(j):
        for other in range(1, dp):
            y_arrival(other, j).wait_recv()
        total = parts[0, j]
        for r in range(1, dp):
            total = total + parts[r, j]
        gate_pre = total[:, 0:hid]
        up_pre = total[:, hid : 2 * hid]
        grad_hid = total[:, 2 * hid : 3 * hid]
        real = lax.broadcasted_iota(jnp.int32, (rows, hid), 0) < cap
        weight = jnp.concatenate(
            [to_col(p_in[2 * j][0:1, :], rows), to_col(p_in[2 * j + 1][0:1, :], rows)], axis=0
        )
        sig = jax.nn.sigmoid(gate_pre)
        silu_out = gate_pre * sig
        slope = sig * (1.0 + gate_pre * (1.0 - sig))
        hidden = silu_out * up_pre
        scaled = weight * grad_hid
        products = hidden * grad_hid
        scores = []
        for b in range(2):
            here = slice(b * rows, (b + 1) * rows)

            def spread(value):
                value = jnp.where(real, value[here], 0.0)
                return jnp.concatenate([value, jnp.zeros((pair - rows, hid), F32)], axis=0)

            k = 2 * j + b
            rows_a[k, :, 0:hid] = spread(scaled * up_pre * slope).astype(BF16)
            rows_a[k, :, hid : 2 * hid] = spread(scaled * silu_out).astype(BF16)
            rows_a[k, :, 2 * hid : 3 * hid] = pltpu.roll(
                spread(weight * hidden), cap, 0
            ).astype(BF16)
            col = jnp.sum(jnp.where(real, products[here], 0.0), axis=1, keepdims=True)
            scores.append(jnp.broadcast_to(to_row(col), s_out.shape[1:]))
        return scores

    def finish(j):
        p_copy(2 * j).wait_recv()
        p_copy(2 * j + 1).wait_recv()
        scores = combine_rows(j)
        for b in range(2):
            s_out[2 * j + b] = scores[b]
            s_copy(2 * j + b).start()

    def step(j, _):
        msg_copy(2 * j).wait_recv()
        msg_copy(2 * j + 1).wait_recv()
        project(j)
        finish(j - 1)
        return 0

    def out_copy(j, c):
        at = pl.ds(pl.multiple_of(c * tile, tile), tile)
        return pltpu.make_async_copy(
            staged.at[j, :, at], (gate_ref, up_ref, down_ref)[j].at[0, :, at], o_sem.at[j, c]
        )

    def outer(lo, hi, opening, closing):
        depth = (hi - lo) * pair
        turned = rows_a[lo:hi].reshape(depth, 3 * hid).T

        def columns(c, _):
            at = pl.ds(pl.multiple_of(c * tile, tile), tile)
            new = jnp.dot(
                turned, recv[lo:hi, :, at].reshape(depth, tile), preferred_element_type=F32
            )
            if not opening:
                new = new + acc[:, at]
            if closing:
                for j in range(3):
                    staged[j, :, at] = new[j * hid : (j + 1) * hid].astype(BF16)
                    out_copy(j, c).start()
            else:
                acc[:, at] = new
            return 0

        lax.fori_loop(0, width // tile, columns, 0)

    msg_copy(1).wait_recv()
    project(0)
    msg_copy(2).wait_recv()
    msg_copy(3).wait_recv()
    project(1)
    p_copy(1).wait_recv()
    scores = combine_rows(0)
    s_in[0] = scores[0]
    s_out[1] = scores[1]
    s_copy(1).start()
    done, j = 0, 2
    for bound in groups:
        upto = min(bound // 2 + 1, half)
        lax.fori_loop(j, upto, step, 0)
        j = upto
        if bound == n:
            finish(half - 1)
        outer(done, bound, done == 0, bound == n)
        done = bound

    def gather_scores(k, carry):
        one, two = carry
        spot = lax.broadcasted_iota(jnp.int32, (rows, tok_count), 0)
        spot = jnp.where(spot < cap, spot + towards(k)[0] * cap, -1)
        col = to_col(s_in[k][0:1, :], rows)
        one = one + jnp.sum(jnp.where(slots_ref[0:1, :] == spot, col, 0.0), axis=0, keepdims=True)
        two = two + jnp.sum(jnp.where(slots_ref[1:2, :] == spot, col, 0.0), axis=0, keepdims=True)
        return one, two

    def arrived(k, carry):
        s_copy(k).wait_recv()
        return gather_scores(k, carry)

    zero = jnp.zeros((1, tok_count), F32)
    one, two = lax.fori_loop(1, n, arrived, gather_scores(0, (zero, zero)))
    comb_ref[0:1, :] = one
    comb_ref[1:2, :] = two

    def drain(k, _):
        msg_copy(k).wait_send()
        p_copy(k).wait_send()
        s_copy(k).wait_send()
        return 0

    lax.fori_loop(1, n, drain, 0)

    def drain_parts(j, _):
        for other in range(1, dp):
            y_copy(other, j).wait_send()
        return 0

    lax.fori_loop(0, half, drain_parts, 0)

    def drain_out(c, _):
        for j in range(3):
            out_copy(j, c).wait()
        return 0

    lax.fori_loop(0, width // tile, drain_out, 0)


def local(n, dp, tokens, grad_out, combine, routes, w_gate, w_up, w_down):
    tok_count, width = tokens.shape
    hid = w_gate.shape[1]
    top_count = routes.shape[1]
    cap = max(2, (9 * tok_count * top_count + 8 * n - 1) // (8 * n))
    pair = round_up(2 * cap, 8)
    rows = round_up(cap, 8)
    tile = 512 if width % 512 == 0 else 256
    grad_shape = jax.ShapeDtypeStruct((1, hid, width), BF16)
    vmem = pl.BlockSpec(memory_space=pltpu.VMEM)
    hbm = pl.BlockSpec(memory_space=pl.ANY)
    dma = pltpu.SemaphoreType.DMA
    gate, up, down, comb = pl.pallas_call(
        functools.partial(kernel, n, dp, cap, tile, (n // 2, n - 2, n)),
        out_shape=(
            grad_shape, grad_shape, grad_shape,
            jax.ShapeDtypeStruct((top_count, tok_count), F32),
        ),
        in_specs=[vmem] * 4 + [hbm] * 3,
        out_specs=(hbm, hbm, hbm, vmem),
        scratch_shapes=[
            pltpu.VMEM((top_count, tok_count), jnp.int32),
            pltpu.VMEM((n, pair, width), BF16),
            pltpu.VMEM((n, pair, width), BF16),
            pltpu.VMEM((3, hid, width), BF16),
            pltpu.VMEM((width, 3 * hid), BF16),
            pltpu.VMEM((n, pair, 3 * hid), BF16),
            pltpu.VMEM((3 * hid, width), F32),
            pltpu.VMEM((dp, n // 2, 2 * rows, 3 * hid), F32),
            pltpu.VMEM((n, 8, 128), F32),
            pltpu.VMEM((n, 8, 128), F32),
            pltpu.VMEM((n, 8, 128), F32),
            pltpu.VMEM((n, 8, 128), F32),
            dma((3,)),
            dma((n,)), dma((n,)), dma((n,)), dma((n,)), dma((n,)), dma((n,)),
            dma((dp, n // 2)), dma((dp, n // 2)), dma((3, width // tile)),
        ],
        compiler_params=pltpu.CompilerParams(
            collective_id=0, has_side_effects=True, vmem_limit_bytes=47 * 1024 * 1024
        ),
        cost_estimate=pl.CostEstimate(
            flops=12 * n * cap * hid * width, bytes_accessed=20 * hid * width, transcendentals=0
        ),
    )(routes.T, combine.T, tokens, grad_out, w_gate, w_up, w_down)
    return gate, up, down, comb.T


def solution(mesh):
    placed = (
        P("expert", "dp"),
        P("expert", "dp"),
        P("expert", None),
        P("expert", None),
        P("expert", None, "dp"),
        P("expert", None, "dp"),
        P("expert", None, "dp"),
    )
    return jax.shard_map(
        functools.partial(local, mesh.shape["expert"], mesh.shape["dp"]),
        mesh=mesh,
        in_specs=placed,
        out_specs=(
            P("expert", None, "dp"),
            P("expert", None, "dp"),
            P("expert", None, "dp"),
            P("expert", None),
        ),
        check_vma=False,
    )
```

```python
import functools

import jax
import jax.numpy as jnp
from jax import lax
from jax.experimental import pallas as pl
from jax.experimental.pallas import tpu as pltpu
from jax.sharding import PartitionSpec as P

MESH = pl.DeviceIdType.MESH
F32 = jnp.float32
BF16 = jnp.bfloat16


def round_up(value, unit):
    return (value + unit - 1) // unit * unit


def partner_of(me, k, n):
    out, bit = 0, 1
    while bit < n:
        out = out + (me // bit + k // bit) % 2 * bit
        bit *= 2
    return out


def diagonal(rows):
    return lax.broadcasted_iota(jnp.int32, (rows, 128), 0) == lax.broadcasted_iota(
        jnp.int32, (rows, 128), 1
    )


def to_row(col):
    rows = col.shape[0]
    return jnp.sum(jnp.where(diagonal(rows), col, 0.0), axis=0, keepdims=True)


def to_col(row, rows):
    return jnp.sum(jnp.where(diagonal(rows), row, 0.0), axis=1, keepdims=True)


def kernel(
    n, dp, cap, tile, groups,
    routes_ref, prob_ref, tok_ref, dy_ref, wg_ref, wu_ref, wd_ref,
    gate_ref, up_ref, down_ref, comb_ref,
    slots_ref, msg, recv, staged, w_all, rows_a, acc, parts, p_out, p_in, s_out, s_in,
    w_sem, m_send, m_recv, p_send, p_recv, s_send, s_recv, y_send, y_recv, o_sem,
):
    me = lax.axis_index("expert")
    mine = lax.axis_index("dp")
    tok_count, width = tok_ref.shape
    hid = wg_ref.shape[1]
    pair = msg.shape[1]
    rows = parts.shape[2] // 2
    half = n // 2

    def towards(k):
        return (partner_of(me, k, n), mine)

    def w_copy(i):
        src = (wg_ref, wu_ref, wd_ref)[i]
        return pltpu.make_async_copy(src.at[0], staged.at[i], w_sem.at[i])

    for i in range(3):
        w_copy(i).start()

    barrier = pltpu.get_barrier_semaphore()

    def greet(k, _):
        pl.semaphore_signal(
            barrier, inc=1, device_id=(partner_of(me, k, n), mine), device_id_type=MESH
        )
        return 0

    lax.fori_loop(1, n, greet, 0)
    for j in range(1, dp):
        pl.semaphore_signal(
            barrier, inc=1, device_id=(me, (mine + j) % dp), device_id_type=MESH
        )
    pl.semaphore_wait(barrier, n - 1 + dp - 1)

    def msg_copy(q):
        return pltpu.make_async_remote_copy(
            src_ref=msg.at[q], dst_ref=recv.at[q], send_sem=m_send.at[q], recv_sem=m_recv.at[q],
            device_id=towards(q), device_id_type=MESH,
        )

    def p_copy(q):
        return pltpu.make_async_remote_copy(
            src_ref=p_out.at[q], dst_ref=p_in.at[q], send_sem=p_send.at[q], recv_sem=p_recv.at[q],
            device_id=towards(q), device_id_type=MESH,
        )

    def s_copy(q):
        return pltpu.make_async_remote_copy(
            src_ref=s_out.at[q], dst_ref=s_in.at[q], send_sem=s_send.at[q], recv_sem=s_recv.at[q],
            device_id=towards(q), device_id_type=MESH,
        )

    def y_copy(j, k):
        return pltpu.make_async_remote_copy(
            src_ref=parts.at[mine, k], dst_ref=parts.at[mine, k],
            send_sem=y_send.at[j, k], recv_sem=y_recv.at[mine, k],
            device_id=(me, (mine + j) % dp), device_id_type=MESH,
        )

    def y_arrival(j, k):
        other = (mine + j) % dp
        return pltpu.make_async_remote_copy(
            src_ref=parts.at[other, k], dst_ref=parts.at[other, k],
            send_sem=y_send.at[j, k], recv_sem=y_recv.at[other, k],
            device_id=(me, other), device_id_type=MESH,
        )

    tokens_by = lax.broadcasted_iota(jnp.int32, (tok_count, tok_count), 0)
    earlier = tokens_by < lax.broadcasted_iota(jnp.int32, (tok_count, tok_count), 1)
    experts = lax.broadcasted_iota(jnp.int32, (round_up(n, 16), tok_count), 0)
    named = [experts == routes_ref[j : j + 1, :] for j in range(2)]
    before = jnp.dot(
        jnp.where(named[0] | named[1], 1.0, 0.0).astype(BF16),
        jnp.where(earlier, 1.0, 0.0).astype(BF16),
        preferred_element_type=F32,
    )
    for j in range(2):
        rank = jnp.sum(jnp.where(named[j], before, 0.0), axis=0, keepdims=True)
        slots_ref[j : j + 1, :] = routes_ref[j : j + 1, :] * cap + rank.astype(jnp.int32)

    def build(k, msg_to, p_to):
        dest = towards(k)[0]
        probs = prob_ref[...].astype(F32)
        place = lax.broadcasted_iota(jnp.int32, (pair, tok_count), 0)
        first = slots_ref[0:1, :] - dest * cap
        second = slots_ref[1:2, :] - dest * cap
        is_x = place < cap
        is_dy = (place >= cap) & (place < 2 * cap)
        pick_x = is_x & ((first == place) | (second == place))
        pick_dy = is_dy & ((first + cap == place) | (second + cap == place))
        picked = jnp.dot(
            jnp.where(pick_x, 1.0, 0.0).astype(BF16), tok_ref[...], preferred_element_type=F32
        ) + jnp.dot(
            jnp.where(pick_dy, 1.0, 0.0).astype(BF16), dy_ref[...], preferred_element_type=F32
        )
        msg_to[k] = picked.astype(BF16)
        spot = lax.broadcasted_iota(jnp.int32, (rows, tok_count), 0)
        prob = jnp.where(first == spot, probs[0:1, :], 0.0) + jnp.where(
            second == spot, probs[1:2, :], 0.0
        )
        p_to[k] = jnp.broadcast_to(
            to_row(jnp.sum(prob, axis=1, keepdims=True)), p_to.shape[1:]
        )

    def start(q):
        p_copy(q).start()
        msg_copy(q).start()

    def send(i, _):
        k = (half + i) % n + i // half
        build(k, msg, p_out)
        start(k)
        return 0

    lax.fori_loop(0, n - 1, send, 0)
    build(0, recv, p_in)
    for i in range(3):
        w_copy(i).wait()

    def turn(c, _):
        at = pl.ds(pl.multiple_of(c * tile, tile), tile)
        for i in range(3):
            w_all[at, i * hid : (i + 1) * hid] = staged[i, :, at].T
        return 0

    lax.fori_loop(0, width // tile, turn, 0)

    def project(j):
        both = jnp.dot(
            recv[pl.ds(2 * j, 2)].reshape(2 * pair, width), w_all[...], preferred_element_type=F32
        )
        held = []
        for b in range(2):
            block = both[b * pair : (b + 1) * pair]
            moved = pltpu.roll(block[:, 2 * hid : 3 * hid], pair - cap, 0)
            held.append(jnp.concatenate([block[0:rows, 0 : 2 * hid], moved[0:rows]], axis=1))
        parts[mine, j] = jnp.concatenate(held, axis=0)
        for other in range(1, dp):
            y_copy(other, j).start()

    def combine_rows(j):
        for other in range(1, dp):
            y_arrival(other, j).wait_recv()
        total = parts[0, j]
        for r in range(1, dp):
            total = total + parts[r, j]
        gate_pre = total[:, 0:hid]
        up_pre = total[:, hid : 2 * hid]
        grad_hid = total[:, 2 * hid : 3 * hid]
        real = lax.broadcasted_iota(jnp.int32, (rows, hid), 0) < cap
        weight = jnp.concatenate(
            [to_col(p_in[2 * j][0:1, :], rows), to_col(p_in[2 * j + 1][0:1, :], rows)], axis=0
        )
        sig = jax.nn.sigmoid(gate_pre)
        silu_out = gate_pre * sig
        slope = sig * (1.0 + gate_pre * (1.0 - sig))
        hidden = silu_out * up_pre
        scaled = weight * grad_hid
        products = hidden * grad_hid
        scores = []
        for b in range(2):
            here = slice(b * rows, (b + 1) * rows)

            def spread(value):
                value = jnp.where(real, value[here], 0.0)
                return jnp.concatenate([value, jnp.zeros((pair - rows, hid), F32)], axis=0)

            k = 2 * j + b
            rows_a[k, :, 0:hid] = spread(scaled * up_pre * slope).astype(BF16)
            rows_a[k, :, hid : 2 * hid] = spread(scaled * silu_out).astype(BF16)
            rows_a[k, :, 2 * hid : 3 * hid] = pltpu.roll(
                spread(weight * hidden), cap, 0
            ).astype(BF16)
            col = jnp.sum(jnp.where(real, products[here], 0.0), axis=1, keepdims=True)
            scores.append(jnp.broadcast_to(to_row(col), s_out.shape[1:]))
        return scores

    def finish(j):
        p_copy(2 * j).wait_recv()
        p_copy(2 * j + 1).wait_recv()
        scores = combine_rows(j)
        for b in range(2):
            s_out[2 * j + b] = scores[b]
            s_copy(2 * j + b).start()

    def step(j, _):
        msg_copy(2 * j).wait_recv()
        msg_copy(2 * j + 1).wait_recv()
        project(j)
        finish(j - 1)
        return 0

    def out_copy(j, c):
        at = pl.ds(pl.multiple_of(c * tile, tile), tile)
        return pltpu.make_async_copy(
            staged.at[j, :, at], (gate_ref, up_ref, down_ref)[j].at[0, :, at], o_sem.at[j, c]
        )

    def outer(lo, hi, opening, closing):
        depth = (hi - lo) * pair
        turned = rows_a[lo:hi].reshape(depth, 3 * hid).T

        def columns(c, _):
            at = pl.ds(pl.multiple_of(c * tile, tile), tile)
            new = jnp.dot(
                turned, recv[lo:hi, :, at].reshape(depth, tile), preferred_element_type=F32
            )
            if not opening:
                new = new + acc[:, at]
            if closing:
                for j in range(3):
                    staged[j, :, at] = new[j * hid : (j + 1) * hid].astype(BF16)
                    out_copy(j, c).start()
            else:
                acc[:, at] = new
            return 0

        lax.fori_loop(0, width // tile, columns, 0)

    msg_copy(1).wait_recv()
    project(0)
    msg_copy(2).wait_recv()
    msg_copy(3).wait_recv()
    project(1)
    p_copy(1).wait_recv()
    scores = combine_rows(0)
    s_in[0] = scores[0]
    s_out[1] = scores[1]
    s_copy(1).start()
    done, j = 0, 2
    for bound in groups:
        upto = min(bound // 2 + 1, half)
        lax.fori_loop(j, upto, step, 0)
        j = upto
        if bound == n:
            finish(half - 1)
        outer(done, bound, done == 0, bound == n)
        done = bound

    def gather_scores(k, carry):
        one, two = carry
        spot = lax.broadcasted_iota(jnp.int32, (rows, tok_count), 0)
        spot = jnp.where(spot < cap, spot + towards(k)[0] * cap, -1)
        col = to_col(s_in[k][0:1, :], rows)
        one = one + jnp.sum(jnp.where(slots_ref[0:1, :] == spot, col, 0.0), axis=0, keepdims=True)
        two = two + jnp.sum(jnp.where(slots_ref[1:2, :] == spot, col, 0.0), axis=0, keepdims=True)
        return one, two

    def arrived(k, carry):
        s_copy(k).wait_recv()
        return gather_scores(k, carry)

    zero = jnp.zeros((1, tok_count), F32)
    one, two = lax.fori_loop(1, n, arrived, gather_scores(0, (zero, zero)))
    comb_ref[0:1, :] = one
    comb_ref[1:2, :] = two

    def drain(k, _):
        msg_copy(k).wait_send()
        p_copy(k).wait_send()
        s_copy(k).wait_send()
        return 0

    lax.fori_loop(1, n, drain, 0)

    def drain_parts(j, _):
        for other in range(1, dp):
            y_copy(other, j).wait_send()
        return 0

    lax.fori_loop(0, half, drain_parts, 0)

    def drain_out(c, _):
        for j in range(3):
            out_copy(j, c).wait()
        return 0

    lax.fori_loop(0, width // tile, drain_out, 0)


def local(n, dp, tokens, grad_out, combine, routes, w_gate, w_up, w_down):
    tok_count, width = tokens.shape
    hid = w_gate.shape[1]
    top_count = routes.shape[1]
    cap = max(2, (9 * tok_count * top_count + 8 * n - 1) // (8 * n))
    pair = round_up(2 * cap, 8)
    rows = round_up(cap, 8)
    tile = 512 if width % 512 == 0 else 256
    grad_shape = jax.ShapeDtypeStruct((1, hid, width), BF16)
    vmem = pl.BlockSpec(memory_space=pltpu.VMEM)
    hbm = pl.BlockSpec(memory_space=pl.ANY)
    dma = pltpu.SemaphoreType.DMA
    gate, up, down, comb = pl.pallas_call(
        functools.partial(kernel, n, dp, cap, tile, (n // 2, n - 2, n)),
        out_shape=(
            grad_shape, grad_shape, grad_shape,
            jax.ShapeDtypeStruct((top_count, tok_count), F32),
        ),
        in_specs=[vmem] * 4 + [hbm] * 3,
        out_specs=(hbm, hbm, hbm, vmem),
        scratch_shapes=[
            pltpu.VMEM((top_count, tok_count), jnp.int32),
            pltpu.VMEM((n, pair, width), BF16),
            pltpu.VMEM((n, pair, width), BF16),
            pltpu.VMEM((3, hid, width), BF16),
            pltpu.VMEM((width, 3 * hid), BF16),
            pltpu.VMEM((n, pair, 3 * hid), BF16),
            pltpu.VMEM((3 * hid, width), F32),
            pltpu.VMEM((dp, n // 2, 2 * rows, 3 * hid), F32),
            pltpu.VMEM((n, 8, 128), F32),
            pltpu.VMEM((n, 8, 128), F32),
            pltpu.VMEM((n, 8, 128), F32),
            pltpu.VMEM((n, 8, 128), F32),
            dma((3,)),
            dma((n,)), dma((n,)), dma((n,)), dma((n,)), dma((n,)), dma((n,)),
            dma((dp, n // 2)), dma((dp, n // 2)), dma((3, width // tile)),
        ],
        compiler_params=pltpu.CompilerParams(
            collective_id=0, has_side_effects=True, vmem_limit_bytes=47 * 1024 * 1024
        ),
        cost_estimate=pl.CostEstimate(
            flops=12 * n * cap * hid * width, bytes_accessed=20 * hid * width, transcendentals=0
        ),
    )(routes.T, combine.T, tokens, grad_out, w_gate, w_up, w_down)
    return gate, up, down, comb.T


def solution(mesh):
    placed = (
        P("expert", "dp"),
        P("expert", "dp"),
        P("expert", None),
        P("expert", None),
        P("expert", None, "dp"),
        P("expert", None, "dp"),
        P("expert", None, "dp"),
    )
    return jax.shard_map(
        functools.partial(local, mesh.shape["expert"], mesh.shape["dp"]),
        mesh=mesh,
        in_specs=placed,
        out_specs=(
            P("expert", None, "dp"),
            P("expert", None, "dp"),
            P("expert", None, "dp"),
            P("expert", None),
        ),
        check_vma=False,
    )
```
